32 devices in a mesh: line: 16 (over z, y, x), tile: 2 (over core).
Axes of the slice: x: 2, y: 2, z: 4, core: 2. Of those that a mesh axis runs over, the one named last changes fastest.
Arguments:
- traces: bfloat16 [8192, 2048], P(('line', 'tile')), may hold values from -6 to 6
- trace_line: int32 [8192], P(('line', 'tile')), may hold values from 0 to 15, as said below
- trace_bin: int32 [8192], P(('line', 'tile')), may hold values from 0 to 127, as said below
- block_offset: int32 [64], P(('line', 'tile')), may hold values from 0 to 3
- nmo_coef: bfloat16 [16, 4, 8, 2048], P('line'), may hold values from -4 to 4
- band_shift: int32 [16, 4, 2048], P('line'), may hold values from 0 to 120
- bandpass: float32 [31, 2048], replicated, may hold values from -1 to 1
- fold: int32 [16, 128], P('line', 'tile'), may hold values from 4 to 20
Outputs:
- stack: float32 [16, 128, 2048], P('line', 'tile')
The draws below stay inside these ranges and needn't reach their ends.
Inputs may be any that keep to these rules, and one draw needn't show every extreme that they name: `trace_line`: of one reader device's 256 traces at most 32 go to one line, and in every draw each device sends exactly 32 to some line. `trace_bin`: the bins of a line form 2 tiles of 64 consecutive bins; of one reader device's traces at most 16 go to one tile of one line, and in every draw each device sends exactly 16 to some tile of some line.
All inputs are finite; a program needn't handle non-finite values.
Results may differ from the reference program's by a relative error of at most 0.0003.
Values may be sent and summed in bfloat16 or wider, within the bound.
A program may use at most 64 MiB of HBM per device.

```python
import jax
import jax.numpy as jnp
from jax import lax

NT = 2048
BLK = 128
NOFF = 4
BW = 8
SHIFT = 120
FL = 31
BINS = 128
TR_DEV = 256
TRACES = 8192
CAP = 32
CAPT = 16
BIN_TILE = 64
LINES = 16
N_LINE = 16
N_TILE = 2


def geometry(key):
    readers = N_LINE * N_TILE
    cells = N_LINE * CAP
    heavy = jax.random.randint(jax.random.fold_in(key, 11), (N_LINE,), 0, 4)

    def one_reader(reader_key):
        key_a, key_b, key_c, key_d, key_e = jax.random.split(reader_key, 5)
        forced = jax.random.randint(key_a, (), 0, N_LINE)
        noise = jax.random.randint(key_b, (N_LINE, CAP), 0, 4096)
        line_grid = jnp.broadcast_to(jnp.arange(N_LINE, dtype=jnp.int32)[:, None], (N_LINE, CAP))
        score = noise * (1 + heavy[:, None]) + jnp.where(line_grid == forced, 16384, 0)
        score = score.reshape(-1) * cells + jnp.arange(cells, dtype=jnp.int32)
        chosen = lax.top_k(score, TR_DEV)[1]
        chosen = chosen[jax.random.permutation(key_c, TR_DEV)]
        line_index = chosen // CAP
        slot_index = chosen % CAP
        tile_orders = jax.vmap(lambda line_key: jax.random.permutation(line_key, N_TILE))(jax.random.split(key_d, N_LINE))
        tile_index = tile_orders[line_index, slot_index // CAPT]
        within = jax.random.randint(key_e, (TR_DEV,), 0, BIN_TILE)
        return (line_index, tile_index * BIN_TILE + within)
    keys = jax.random.split(jax.random.fold_in(key, 5), readers)
    lines, bins_drawn = jax.vmap(one_reader)(keys)
    return (lines.reshape(-1).astype(jnp.int32), bins_drawn.reshape(-1).astype(jnp.int32))


def draw_trace_line(key, part):
    return geometry(key)[0]


def draw_trace_bin(key, part):
    return geometry(key)[1]


def with_ends(entries, key, low, largest):
    longest = entries.shape.index(max(entries.shape))
    spots = []
    for shift in (0, 1):
        where = [jax.random.randint(jax.random.fold_in(key, axis), (), 0, length) for axis, length in enumerate(entries.shape)]
        where[longest] = (where[longest] + shift) % entries.shape[longest]
        spots.append(tuple(where))
    return entries.at[spots[0]].set(low).at[spots[1]].set(largest)


def block_levels(own_key, shape, pieces, low, high):
    loudness, own = 1.0, jax.random.fold_in(own_key, 6)
    for dim, blocks in pieces:
        draws = jnp.exp(jax.random.uniform(jax.random.fold_in(own, dim), (blocks,), jnp.float32, low / len(pieces), high / len(pieces)))
        loudness = loudness * jnp.repeat(draws, shape[dim] // blocks).reshape([-1 if axis == dim else 1 for axis in range(len(shape))])
    return loudness


def gaussian(own_key, extent, width, reach, cuts=(), kind=jnp.bfloat16):
    entries = width * jax.random.normal(own_key, extent, jnp.float32)
    if cuts:
        entries = entries * block_levels(own_key, extent, cuts, -0.22, 0.18)
    return jnp.clip(entries, -reach, reach).astype(kind)


def setup_inputs(seed: int = 0) -> dict:
    seeds = jax.random.split(jax.random.key(seed), 9)
    traces = gaussian(seeds[0], (TRACES, NT), 1.0, 6.0, ((0, 32),))
    trace_line = draw_trace_line(jax.random.fold_in(seeds[8], 71), 0)
    trace_bin = draw_trace_bin(jax.random.fold_in(seeds[8], 71), 0)
    block_offset = with_ends(jax.random.randint(seeds[3], (TRACES // BLK,), 0, NOFF), jax.random.fold_in(seeds[3], 1), 0, NOFF - 1).astype(jnp.int32)
    nmo_coef = gaussian(seeds[4], (LINES, NOFF, BW, NT), 0.6, 4.0, ((0, 16),))
    band_shift = with_ends(jax.random.randint(seeds[5], (LINES, NOFF, NT), 0, SHIFT + 1), jax.random.fold_in(seeds[5], 1), 0, SHIFT).astype(jnp.int32)
    bandpass = gaussian(seeds[6], (FL, NT), FL ** -0.5, 1.0, (), jnp.float32)
    fold = with_ends(jax.random.randint(seeds[7], (LINES, BINS), 4, 21), jax.random.fold_in(seeds[7], 1), 4, 20).astype(jnp.int32)
    return {"traces": traces, "trace_line": trace_line, "trace_bin": trace_bin, "block_offset": block_offset, "nmo_coef": nmo_coef, "band_shift": band_shift, "bandpass": bandpass, "fold": fold}


def reference(traces, trace_line, trace_bin, block_offset, nmo_coef, band_shift, bandpass, fold):
    block_total = block_offset.shape[0]
    blocks = traces.reshape(block_total, BLK, NT)
    line_blocks = trace_line.reshape(block_total, BLK)
    bin_blocks = trace_bin.reshape(block_total, BLK)
    tap_iota = jnp.arange(BW, dtype=jnp.int32)
    sample_iota = jnp.arange(NT, dtype=jnp.int32)

    def step(total, items):
        block, line_ids, bin_ids, offset_class = items
        weights = nmo_coef[line_ids, offset_class].astype(jnp.float32)
        shifts = band_shift[line_ids, offset_class].astype(jnp.int32)
        index = sample_iota[None, None, :] + shifts[:, None, :] + tap_iota[None, :, None]
        padded = jnp.concatenate([block.astype(jnp.float32), jnp.zeros((BLK, 128), jnp.float32)], 1)
        spread = jnp.broadcast_to(padded[:, None, :], (BLK, BW, NT + 128))
        values = jnp.take_along_axis(spread, index.astype(jnp.int32), axis=2)
        corrected = jnp.sum(weights * values, axis=1)
        total = total.at[(line_ids * BINS + bin_ids).astype(jnp.int32)].add(corrected)
        return total, None

    start = jnp.zeros((N_LINE * BINS, NT), jnp.float32)
    gathered, _ = lax.scan(step, start, (blocks, line_blocks, bin_blocks, block_offset))
    half = (FL - 1) // 2
    padded_stack = jnp.concatenate([jnp.zeros((N_LINE * BINS, half), jnp.float32), gathered, jnp.zeros((N_LINE * BINS, FL - 1 - half), jnp.float32)], 1)
    filtered = jnp.zeros((N_LINE * BINS, NT), jnp.float32)
    for tap_index in range(FL):
        filtered = filtered + bandpass[tap_index][None, :] * padded_stack[:, tap_index:tap_index + NT]
    result = filtered / fold.reshape(-1).astype(jnp.float32)[:, None]
    return result.reshape(N_LINE, BINS, NT)
```

```python
import functools

import jax
import jax.numpy as jnp
from jax import lax
from jax.experimental import pallas as pl
from jax.experimental.pallas import tpu as pltpu
from jax.sharding import PartitionSpec as P

LANES = 128
CHUNK = 128
MESH = pl.DeviceIdType.MESH


def iota(shape, dim):
    return lax.broadcasted_iota(jnp.int32, shape, dim)


def to_column(row):
    n = row.shape[1]
    wide = jnp.broadcast_to(row, (n, n))
    return jnp.sum(jnp.where(iota((n, n), 0) == iota((n, n), 1), wide, 0.0), 1, keepdims=True)


def dot(a, b):
    return jnp.dot(a, b, preferred_element_type=jnp.float32)


def split(value):
    high = value.astype(jnp.bfloat16)
    low = (value - high.astype(jnp.float32)).astype(jnp.bfloat16)
    return high, low


def kernel(
    n_line, n_tile, cap, noff, taps,
    traces, line_ref, bin_ref, block_ref, coef, shift, band, fold_ref,
    out,
    packed, landed, total, halves, nmo, bp_high, bp_low, shifted,
    send_sem, recv_sem,
):
    n = n_line * n_tile
    me = lax.axis_index("line") * n_tile + lax.axis_index("tile")
    trace_count, length = traces.shape
    share = out.shape[0]
    ids = noff * share
    groups = length // LANES
    per_chunk = CHUNK // cap
    chunks = n // per_chunk
    filter_taps = band.shape[0]
    half = (filter_taps - 1) // 2

    def place(index):
        return (index // n_tile, index % n_tile)

    barrier = pltpu.get_barrier_semaphore()

    @pl.loop(1, n)
    def _(k):
        pl.semaphore_signal(barrier, inc=1, device_id=place((me + k) % n), device_id_type=MESH)

    bins = bin_ref[...]
    tile = jnp.zeros_like(bins)
    for t in range(1, n_tile):
        tile = tile + jnp.where(bins >= t * share, 1, 0)
    offset = line_ref[...] * n_tile + tile - me
    offset = jnp.where(offset < 0, offset + n, offset).astype(jnp.float32)
    same = (to_column(offset) == offset) & (
        iota((trace_count, trace_count), 0) < iota((trace_count, trace_count), 1)
    )
    rank = jnp.sum(jnp.where(same, 1.0, 0.0), 0, keepdims=True)
    slot = offset * cap + rank
    block = trace_count // block_ref.shape[0]
    spot = iota((1, trace_count), 1)
    trace_class = jnp.zeros((1, trace_count), jnp.int32)
    for b in range(block_ref.shape[0]):
        inside = (spot >= b * block) & (spot < (b + 1) * block)
        trace_class = jnp.where(inside, block_ref[b], trace_class)
    ident = (trace_class * share + bins - tile * share).astype(jnp.float32)
    ident = jnp.broadcast_to(to_column(ident), (trace_count, LANES)).astype(jnp.bfloat16)

    def pack(chunk):
        base = chunk * CHUNK
        rows = (iota((CHUNK, trace_count), 0) + base).astype(jnp.float32)
        pick = jnp.where(rows == slot, 1.0, 0.0).astype(jnp.bfloat16)
        width = 512

        @pl.loop(0, length // width)
        def _(j):
            cols = pl.ds(pl.multiple_of(j * width, width), width)
            packed[pl.ds(base, CHUNK), cols] = dot(pick, traces[:, cols]).astype(jnp.bfloat16)

        packed[pl.ds(base, CHUNK), pl.ds(length, LANES)] = dot(pick, ident).astype(jnp.bfloat16)

    def copy(k):
        rows = pl.ds(pl.multiple_of(k * cap, cap), cap)
        return pltpu.make_async_remote_copy(
            src_ref=packed.at[rows],
            dst_ref=landed.at[rows],
            send_sem=send_sem.at[k],
            recv_sem=recv_sem.at[k],
            device_id=place((me + k) % n),
            device_id_type=MESH,
        )

    order = sorted(range(chunks), key=lambda c: abs(c * per_chunk - n // 2))
    for number, chunk in enumerate(order):
        pack(chunk)
        if number == 0:
            pl.semaphore_wait(barrier, n - 1)

        @pl.loop(max(chunk * per_chunk, 1), (chunk + 1) * per_chunk)
        def _(k):
            copy(k).start()

        if chunk == 0:
            landed[0:cap] = packed[0:cap]

    position = iota((2 * LANES, LANES), 0) - iota((2 * LANES, LANES), 1)

    @pl.loop(0, groups)
    def _(g):
        cols = pl.ds(pl.multiple_of(g * LANES, LANES), LANES)
        for c in range(noff):
            place_rel = position - shift[c : c + 1, cols]
            weights = coef[c * taps : (c + 1) * taps, cols].astype(jnp.float32)
            matrix = jnp.zeros((2 * LANES, LANES), jnp.float32)
            for b in range(taps):
                matrix = jnp.where(place_rel == b, weights[b : b + 1], matrix)
            nmo[g * noff + c] = matrix.astype(jnp.bfloat16)
        matrix = jnp.zeros((2 * LANES, LANES), jnp.float32)
        for b in range(filter_taps):
            matrix = jnp.where(position == LANES // 2 + b - half, band[b : b + 1, cols], matrix)
        high, low = split(matrix)
        bp_high[g] = high
        bp_low[g] = low

    for c in range(noff):
        halves[c, :, pl.ds(length, LANES)] = jnp.zeros((2 * share, LANES), jnp.bfloat16)
    scale = 1.0 / to_column(fold_ref[...].astype(jnp.float32))

    for number, chunk in enumerate(order):

        @pl.loop(max(chunk * per_chunk, 1), (chunk + 1) * per_chunk)
        def _(k):
            copy(k).wait_recv()

        base = chunk * CHUNK
        names = landed[pl.ds(base, CHUNK), pl.ds(length, LANES)].astype(jnp.float32)
        names = jnp.transpose(names)[0:1, :]
        chosen = jnp.where(iota((ids, CHUNK), 0).astype(jnp.float32) == names, 1.0, 0.0)
        chosen = chosen.astype(jnp.bfloat16)
        width = 256

        @pl.loop(0, length // width)
        def _(j):
            cols = pl.ds(pl.multiple_of(j * width, width), width)
            part = dot(chosen, landed[pl.ds(base, CHUNK), cols])
            if number > 0:
                part = part + total[:, cols]
            if number < chunks - 1:
                total[:, cols] = part
            else:
                high, low = split(part)
                for c in range(noff):
                    halves[c, 0:share, cols] = high[c * share : (c + 1) * share]
                    halves[c, share : 2 * share, cols] = low[c * share : (c + 1) * share]

    left = iota((share, LANES), 1) < LANES // 2

    def store_shifted(g, value):
        high, low = split(value)
        cols = pl.ds(g * LANES, LANES)
        shifted[0:share, cols] = high
        shifted[share : 2 * share, cols] = low

    def bandpass(g):
        window = shifted[:, pl.ds(g * LANES, 2 * LANES)]
        first = dot(window, bp_high[g])
        second = dot(window[0:share], bp_low[g])
        out[:, pl.ds(g * LANES, LANES)] = (first[0:share] + first[share:] + second) * scale

    before = jnp.zeros((share, LANES), jnp.float32)
    for g in range(groups):
        acc = dot(halves[0, :, pl.ds(g * LANES, 2 * LANES)], nmo[g * noff])
        for c in range(1, noff):
            acc = acc + dot(halves[c, :, pl.ds(g * LANES, 2 * LANES)], nmo[g * noff + c])
        turned = pltpu.roll(acc[0:share] + acc[share:], LANES // 2, 1)
        store_shifted(g, jnp.where(left, before, turned))
        before = turned
        if g >= 1:
            bandpass(g - 1)
    store_shifted(groups, jnp.where(left, before, 0.0))
    bandpass(groups - 1)

    @pl.loop(1, n)
    def _(k):
        copy(k).wait_send()


def body(traces, trace_line, trace_bin, block_offset, nmo_coef, band_shift, bandpass, fold):
    n_line = lax.axis_size("line")
    n_tile = lax.axis_size("tile")
    n = n_line * n_tile
    trace_count, length = traces.shape
    share = fold.shape[1]
    noff, taps = nmo_coef.shape[1:3]
    groups = length // LANES
    cap = -(-(2 * trace_count // n) // 16) * 16
    rows = n * cap
    vmem = pl.BlockSpec(memory_space=pltpu.VMEM)
    result = pl.pallas_call(
        functools.partial(kernel, n_line, n_tile, cap, noff, taps),
        out_shape=jax.ShapeDtypeStruct((share, length), jnp.float32),
        in_specs=[vmem, vmem, vmem, pl.BlockSpec(memory_space=pltpu.SMEM), vmem, vmem, vmem, vmem],
        out_specs=vmem,
        scratch_shapes=[
            pltpu.VMEM((rows, length + LANES), jnp.bfloat16),
            pltpu.VMEM((rows, length + LANES), jnp.bfloat16),
            pltpu.VMEM((noff * share, length), jnp.float32),
            pltpu.VMEM((noff, 2 * share, length + LANES), jnp.bfloat16),
            pltpu.VMEM((groups * noff, 2 * LANES, LANES), jnp.bfloat16),
            pltpu.VMEM((groups, 2 * LANES, LANES), jnp.bfloat16),
            pltpu.VMEM((groups, 2 * LANES, LANES), jnp.bfloat16),
            pltpu.VMEM((2 * share, length + LANES), jnp.bfloat16),
            pltpu.SemaphoreType.DMA((n,)),
            pltpu.SemaphoreType.DMA((n,)),
        ],
        compiler_params=pltpu.CompilerParams(
            collective_id=0, has_side_effects=True, vmem_limit_bytes=50 * 1024 * 1024
        ),
        name="route_and_stack",
    )(
        traces,
        trace_line.reshape(1, -1),
        trace_bin.reshape(1, -1),
        block_offset,
        nmo_coef.reshape(noff * taps, length),
        band_shift.reshape(noff, length),
        bandpass,
        fold,
    )
    return result[None]


def solution(mesh):
    placed = (
        P(("line", "tile"), None),
        P(("line", "tile")),
        P(("line", "tile")),
        P(("line", "tile")),
        P("line", None, None, None),
        P("line", None, None),
        P(),
        P("line", "tile"),
    )
    return jax.shard_map(
        body, mesh=mesh, in_specs=placed, out_specs=P("line", "tile", None), check_vma=False
    )
```

```python
import functools

import jax
import jax.numpy as jnp
from jax import lax
from jax.experimental import pallas as pl
from jax.experimental.pallas import tpu as pltpu
from jax.sharding import PartitionSpec as P

LANES = 128
CHUNK = 128
PARTS = 2
MESH = pl.DeviceIdType.MESH


def iota(shape, dim):
    return lax.broadcasted_iota(jnp.int32, shape, dim)


def to_column(row):
    n = row.shape[1]
    wide = jnp.broadcast_to(row, (n, n))
    return jnp.sum(jnp.where(iota((n, n), 0) == iota((n, n), 1), wide, 0.0), 1, keepdims=True)


def dot(a, b):
    return jnp.dot(a, b, preferred_element_type=jnp.float32)


def split(value):
    high = value.astype(jnp.bfloat16)
    low = (value - high.astype(jnp.float32)).astype(jnp.bfloat16)
    return high, low


def kernel(
    n_line, n_tile, cap, noff, taps,
    traces_hbm, line_hbm, bin_hbm, block_hbm, coef_hbm, shift_hbm, band_hbm, fold_hbm,
    out,
    traces, line_ref, bin_ref, block_ref, coef, shift, band, fold_ref,
    pick, packed, landed, names_out, names_in, chosen, halves, nmo, bp_high, bp_low, shifted,
    local_sem, part_sem, send_sem, recv_sem, name_send_sem, name_recv_sem,
):
    n = n_line * n_tile
    me = lax.axis_index("line") * n_tile + lax.axis_index("tile")
    trace_count, length = traces.shape
    rows_total = packed.shape[0]
    share = out.shape[0]
    ids = noff * share
    groups = length // LANES
    per_chunk = CHUNK // cap
    chunks = n // per_chunk
    parts = part_sem.shape[0]
    width = length // parts
    filter_taps = band.shape[0]
    half = (filter_taps - 1) // 2

    small = [
        pltpu.make_async_copy(source, target, local_sem.at[index])
        for index, (source, target) in enumerate(
            [
                (line_hbm, line_ref), (bin_hbm, bin_ref), (block_hbm, block_ref),
                (fold_hbm, fold_ref), (shift_hbm, shift), (coef_hbm, coef), (band_hbm, band),
            ]
        )
    ]
    for item in small[:4]:
        item.start()
    pieces = []
    for p in range(parts):
        cols = pl.ds(p * width, width)
        pieces.append(
            pltpu.make_async_copy(traces_hbm.at[:, cols], traces.at[:, cols], part_sem.at[p])
        )
        pieces[p].start()
    for item in small[4:]:
        item.start()

    def place(index):
        return (index // n_tile, index % n_tile)

    barrier = pltpu.get_barrier_semaphore()

    @pl.loop(1, n)
    def _(k):
        pl.semaphore_signal(barrier, inc=1, device_id=place((me + k) % n), device_id_type=MESH)

    for item in small[:4]:
        item.wait()

    bins = bin_ref[...]
    tile = jnp.zeros_like(bins)
    for t in range(1, n_tile):
        tile = tile + jnp.where(bins >= t * share, 1, 0)
    offset = line_ref[...] * n_tile + tile - me
    offset = jnp.where(offset < 0, offset + n, offset).astype(jnp.float32)
    same = (to_column(offset) == offset) & (
        iota((trace_count, trace_count), 0) < iota((trace_count, trace_count), 1)
    )
    rank = jnp.sum(jnp.where(same, 1.0, 0.0), 0, keepdims=True)
    slot = offset * cap + rank

    for chunk in range(chunks):
        rows = (iota((CHUNK, trace_count), 0) + chunk * CHUNK).astype(jnp.float32)
        pick[pl.ds(chunk * CHUNK, CHUNK), :] = jnp.where(rows == slot, 1.0, 0.0).astype(jnp.bfloat16)

    def copy(p, k):
        rows = pl.ds(pl.multiple_of(k * cap, cap), cap)
        cols = pl.ds(p * width, width)
        return pltpu.make_async_remote_copy(
            src_ref=packed.at[rows, cols],
            dst_ref=landed.at[rows, cols],
            send_sem=send_sem.at[p, k],
            recv_sem=recv_sem.at[p, k],
            device_id=place((me + k) % n),
            device_id_type=MESH,
        )

    def name_copy(k):
        return pltpu.make_async_remote_copy(
            src_ref=names_out.at[pl.ds(k, 1)],
            dst_ref=names_in.at[pl.ds(k, 1)],
            send_sem=name_send_sem.at[k],
            recv_sem=name_recv_sem.at[k],
            device_id=place((me + k) % n),
            device_id_type=MESH,
        )

    def far_first(i):
        return 1 + (i + n // 2 - n // 8) % (n - 1)

    for p in range(parts):
        cols = pl.ds(p * width, width)
        pieces[p].wait()

        @pl.loop(0, chunks)
        def _(chunk):
            rows = pl.ds(pl.multiple_of(chunk * CHUNK, CHUNK), CHUNK)
            packed[rows, cols] = dot(pick[rows, :], traces[:, cols]).astype(jnp.bfloat16)

        if p == 0:
            pl.semaphore_wait(barrier, n - 1)

        @pl.loop(0, n - 1)
        def _(i):
            copy(p, far_first(i)).start()

        landed[0:cap, cols] = packed[0:cap, cols]
        if p == 0:
            block = trace_count // block_ref.shape[1]
            spot = iota((1, trace_count), 1)
            trace_class = jnp.zeros((1, trace_count), jnp.int32)
            for b in range(block_ref.shape[1]):
                inside = (spot >= b * block) & (spot < (b + 1) * block)
                value = jnp.broadcast_to(block_ref[:, b : b + 1], (1, trace_count))
                trace_class = jnp.where(inside, value, trace_class)
            ident = (trace_class * share + bins - tile * share).astype(jnp.float32)
            ident = jnp.broadcast_to(to_column(ident), (trace_count, LANES)).astype(jnp.bfloat16)
            for chunk in range(chunks):
                rows = pl.ds(chunk * CHUNK, CHUNK)
                wide = jnp.transpose(dot(pick[rows, :], ident))[0:per_chunk]
                lane = iota((per_chunk, CHUNK), 1)
                first = iota((per_chunk, CHUNK), 0) * cap
                mine = (lane >= first) & (lane < first + cap)
                names_out[pl.ds(chunk * per_chunk, per_chunk), :] = jnp.where(mine, wide, 0.0)

            @pl.loop(0, n - 1)
            def _(i):
                name_copy(far_first(i)).start()

            names_in[0:1] = names_out[0:1]

    for item in small[4:]:
        item.wait()
    position = iota((2 * LANES, LANES), 0) - iota((2 * LANES, LANES), 1)

    @pl.loop(0, groups)
    def _(g):
        cols = pl.ds(pl.multiple_of(g * LANES, LANES), LANES)
        for c in range(noff):
            place_rel = position - shift[c : c + 1, cols]
            weights = coef[c * taps : (c + 1) * taps, cols].astype(jnp.float32)
            matrix = jnp.zeros((2 * LANES, LANES), jnp.float32)
            for b in range(taps):
                matrix = jnp.where(place_rel == b, weights[b : b + 1], matrix)
            nmo[g * noff + c] = matrix.astype(jnp.bfloat16)
        matrix = jnp.zeros((2 * LANES, LANES), jnp.float32)
        for b in range(filter_taps):
            matrix = jnp.where(position == LANES // 2 + b - half, band[b : b + 1, cols], matrix)
        high, low = split(matrix)
        bp_high[g] = high
        bp_low[g] = low

    for c in range(noff):
        halves[c, :, pl.ds(length, LANES)] = jnp.zeros((2 * share, LANES), jnp.bfloat16)
    scale = 1.0 / to_column(fold_ref[...].astype(jnp.float32))

    @pl.loop(1, n)
    def _(k):
        name_copy(k).wait_recv()

    for chunk in range(chunks):
        row = jnp.sum(names_in[pl.ds(chunk * per_chunk, per_chunk), :], 0, keepdims=True)
        hit = iota((ids, CHUNK), 0).astype(jnp.float32) == row
        chosen[:, pl.ds(chunk * CHUNK, CHUNK)] = jnp.where(hit, 1.0, 0.0).astype(jnp.bfloat16)

    left = iota((share, LANES), 1) < LANES // 2

    def store_shifted(g, value):
        high, low = split(value)
        cols = pl.ds(g * LANES, LANES)
        shifted[0:share, cols] = high
        shifted[share : 2 * share, cols] = low

    def bandpass(g):
        window = shifted[:, pl.ds(g * LANES, 2 * LANES)]
        first = dot(window, bp_high[g])
        second = dot(window[0:share], bp_low[g])
        out[:, pl.ds(g * LANES, LANES)] = (first[0:share] + first[share:] + second) * scale

    before = jnp.zeros((share, LANES), jnp.float32)
    done = 0
    for p in range(parts):

        @pl.loop(1, n)
        def _(k):
            copy(p, k).wait_recv()

        step = 2 * LANES
        for j in range(width // step):
            cols = pl.ds(p * width + j * step, step)
            high, low = split(dot(chosen[...], landed[:, cols]))
            for c in range(noff):
                halves[c, 0:share, cols] = high[c * share : (c + 1) * share]
                halves[c, share : 2 * share, cols] = low[c * share : (c + 1) * share]
        ready = groups if p == parts - 1 else (p + 1) * width // LANES - 1
        for g in range(done, ready):
            acc = dot(halves[0, :, pl.ds(g * LANES, 2 * LANES)], nmo[g * noff])
            for c in range(1, noff):
                acc = acc + dot(halves[c, :, pl.ds(g * LANES, 2 * LANES)], nmo[g * noff + c])
            turned = pltpu.roll(acc[0:share] + acc[share:], LANES // 2, 1)
            store_shifted(g, jnp.where(left, before, turned))
            before = turned
            if g >= 1:
                bandpass(g - 1)
        done = ready
    store_shifted(groups, jnp.where(left, before, 0.0))
    bandpass(groups - 1)

    @pl.loop(1, n)
    def _(k):
        name_copy(k).wait_send()
        for p in range(parts):
            copy(p, k).wait_send()


def body(traces, trace_line, trace_bin, block_offset, nmo_coef, band_shift, bandpass, fold):
    n_line = lax.axis_size("line")
    n_tile = lax.axis_size("tile")
    n = n_line * n_tile
    trace_count, length = traces.shape
    share = fold.shape[1]
    noff, taps = nmo_coef.shape[1:3]
    groups = length // LANES
    cap = -(-(2 * trace_count // n) // 16) * 16
    rows = n * cap
    parts = PARTS
    vmem = pl.BlockSpec(memory_space=pltpu.VMEM)
    hbm = pl.BlockSpec(memory_space=pltpu.HBM)
    result = pl.pallas_call(
        functools.partial(kernel, n_line, n_tile, cap, noff, taps),
        out_shape=jax.ShapeDtypeStruct((share, length), jnp.float32),
        in_specs=[hbm] * 8,
        out_specs=vmem,
        scratch_shapes=[
            pltpu.VMEM((trace_count, length), jnp.bfloat16),
            pltpu.VMEM((1, trace_count), jnp.int32),
            pltpu.VMEM((1, trace_count), jnp.int32),
            pltpu.VMEM((1, block_offset.shape[0]), jnp.int32),
            pltpu.VMEM((noff * taps, length), jnp.bfloat16),
            pltpu.VMEM((noff, length), jnp.int32),
            pltpu.VMEM(bandpass.shape, jnp.float32),
            pltpu.VMEM((1, share), jnp.int32),
            pltpu.VMEM((rows, trace_count), jnp.bfloat16),
            pltpu.VMEM((rows, length), jnp.bfloat16),
            pltpu.VMEM((rows, length), jnp.bfloat16),
            pltpu.VMEM((n, LANES), jnp.float32),
            pltpu.VMEM((n, LANES), jnp.float32),
            pltpu.VMEM((noff * share, rows), jnp.bfloat16),
            pltpu.VMEM((noff, 2 * share, length + LANES), jnp.bfloat16),
            pltpu.VMEM((groups * noff, 2 * LANES, LANES), jnp.bfloat16),
            pltpu.VMEM((groups, 2 * LANES, LANES), jnp.bfloat16),
            pltpu.VMEM((groups, 2 * LANES, LANES), jnp.bfloat16),
            pltpu.VMEM((2 * share, length + LANES), jnp.bfloat16),
            pltpu.SemaphoreType.DMA((7,)),
            pltpu.SemaphoreType.DMA((parts,)),
            pltpu.SemaphoreType.DMA((parts, n)),
            pltpu.SemaphoreType.DMA((parts, n)),
            pltpu.SemaphoreType.DMA((n,)),
            pltpu.SemaphoreType.DMA((n,)),
        ],
        compiler_params=pltpu.CompilerParams(
            collective_id=0, has_side_effects=True, vmem_limit_bytes=60 * 1024 * 1024
        ),
        name="route_and_stack",
    )(
        traces,
        trace_line.reshape(1, -1),
        trace_bin.reshape(1, -1),
        block_offset.reshape(1, -1),
        nmo_coef.reshape(noff * taps, length),
        band_shift.reshape(noff, length),
        bandpass,
        fold,
    )
    return result[None]


def solution(mesh):
    placed = (
        P(("line", "tile"), None),
        P(("line", "tile")),
        P(("line", "tile")),
        P(("line", "tile")),
        P("line", None, None, None),
        P("line", None, None),
        P(),
        P("line", "tile"),
    )
    return jax.shard_map(
        body, mesh=mesh, in_specs=placed, out_specs=P("line", "tile", None), check_vma=False
    )
```

```python
import functools

import jax
import jax.numpy as jnp
from jax import lax
from jax.experimental import pallas as pl
from jax.experimental.pallas import tpu as pltpu
from jax.sharding import PartitionSpec as P

LANES = 128
CHUNK = 128
PARTS = 4
MESH = pl.DeviceIdType.MESH


def iota(shape, dim):
    return lax.broadcasted_iota(jnp.int32, shape, dim)


def to_column(row):
    n = row.shape[1]
    wide = jnp.broadcast_to(row, (n, n))
    return jnp.sum(jnp.where(iota((n, n), 0) == iota((n, n), 1), wide, 0.0), 1, keepdims=True)


def dot(a, b):
    return jnp.dot(a, b, preferred_element_type=jnp.float32)


def split(value):
    high = value.astype(jnp.bfloat16)
    low = (value - high.astype(jnp.float32)).astype(jnp.bfloat16)
    return high, low


def kernel(
    n_line, n_tile, cap, noff, taps,
    traces_hbm, line_hbm, bin_hbm, block_hbm, coef_hbm, shift_hbm, band_hbm, fold_hbm,
    out,
    traces, line_ref, bin_ref, block_ref, coef, shift, band, fold_ref,
    pick, packed, landed, names_out, names_in, chosen, halves, nmo, bp_high, bp_low, shifted,
    coef_in, shift_in, sums_out, sums_in,
    local_sem, part_sem, send_sem, recv_sem, name_send_sem, name_recv_sem,
    far_send_sem, far_recv_sem,
):
    n = n_line * n_tile
    me = lax.axis_index("line") * n_tile + lax.axis_index("tile")
    m = n // 2
    my_half = me // m
    spot_in_half = me % m
    trace_count, length = traces.shape
    share = out.shape[0]
    ids = noff * share
    groups = length // LANES
    per_chunk = CHUNK // cap
    chunks = n // per_chunk
    parts = part_sem.shape[0]
    width = length // parts
    filter_taps = band.shape[0]
    half = (filter_taps - 1) // 2

    small = [
        pltpu.make_async_copy(source, target, local_sem.at[index])
        for index, (source, target) in enumerate(
            [
                (line_hbm, line_ref), (bin_hbm, bin_ref), (block_hbm, block_ref),
                (fold_hbm, fold_ref), (shift_hbm, shift), (coef_hbm, coef), (band_hbm, band),
            ]
        )
    ]
    for item in small[:4]:
        item.start()
    pieces = []
    for p in range(parts):
        cols = pl.ds(p * width, width)
        pieces.append(
            pltpu.make_async_copy(traces_hbm.at[:, cols], traces.at[:, cols], part_sem.at[p])
        )
        pieces[p].start()
    for item in small[4:]:
        item.start()

    def place(index):
        return (index // n_tile, index % n_tile)

    barrier = pltpu.get_barrier_semaphore()

    mirror = place((me + m) % n)

    def peer(k):
        return place(my_half * m + (spot_in_half + k) % m)

    @pl.loop(1, m)
    def _(k):
        pl.semaphore_signal(barrier, inc=1, device_id=peer(k), device_id_type=MESH)

    pl.semaphore_signal(barrier, inc=1, device_id=mirror, device_id_type=MESH)

    for item in small[:4]:
        item.wait()

    bins = bin_ref[...]
    tile = jnp.zeros_like(bins)
    for t in range(1, n_tile):
        tile = tile + jnp.where(bins >= t * share, 1, 0)
    owner = line_ref[...] * n_tile + tile
    owner_half = jnp.where(owner >= m, 1, 0)
    offset = owner - owner_half * m - spot_in_half
    offset = jnp.where(offset < 0, offset + m, offset)
    offset = jnp.where(owner_half == my_half, offset + m, offset).astype(jnp.float32)
    same = (to_column(offset) == offset) & (
        iota((trace_count, trace_count), 0) < iota((trace_count, trace_count), 1)
    )
    rank = jnp.sum(jnp.where(same, 1.0, 0.0), 0, keepdims=True)
    slot = offset * cap + rank

    for chunk in range(chunks):
        rows = (iota((CHUNK, trace_count), 0) + chunk * CHUNK).astype(jnp.float32)
        pick[pl.ds(chunk * CHUNK, CHUNK), :] = jnp.where(rows == slot, 1.0, 0.0).astype(jnp.bfloat16)

    def copy(p, side, k):
        rows = pl.ds(pl.multiple_of((side * m + k) * cap, cap), cap)
        cols = pl.ds(p * width, width)
        return pltpu.make_async_remote_copy(
            src_ref=packed.at[rows, cols],
            dst_ref=landed.at[rows, cols],
            send_sem=send_sem.at[p, side * m + k],
            recv_sem=recv_sem.at[p, side * m + k],
            device_id=peer(k),
            device_id_type=MESH,
        )

    def name_copy(side, k):
        index = side * m + k
        return pltpu.make_async_remote_copy(
            src_ref=names_out.at[pl.ds(index, 1)],
            dst_ref=names_in.at[pl.ds(index, 1)],
            send_sem=name_send_sem.at[index],
            recv_sem=name_recv_sem.at[index],
            device_id=peer(k),
            device_id_type=MESH,
        )

    def far_copy(index, source, target):
        return pltpu.make_async_remote_copy(
            src_ref=source,
            dst_ref=target,
            send_sem=far_send_sem.at[index],
            recv_sem=far_recv_sem.at[index],
            device_id=mirror,
            device_id_type=MESH,
        )

    far_weights = [far_copy(parts, shift, shift_in), far_copy(parts + 1, coef, coef_in)]

    ends = [(p + 1) * width // LANES - 1 for p in range(parts - 1)] + [groups]
    starts = [0] + ends[:-1]
    far_sums = []
    for p in range(parts):
        cols = pl.ds(starts[p] * LANES, (ends[p] - starts[p]) * LANES)
        far_sums.append(far_copy(p, sums_out.at[:, cols], sums_in.at[:, cols]))

    def turn(i):
        return 1 + (i + m // 2 - 1) % (m - 1)

    def start_part(side, p):
        cols = pl.ds(p * width, width)

        @pl.loop(0, chunks // 2)
        def _(chunk):
            rows = pl.ds(pl.multiple_of((side * (chunks // 2) + chunk) * CHUNK, CHUNK), CHUNK)
            packed[rows, cols] = dot(pick[rows, :], traces[:, cols]).astype(jnp.bfloat16)

        if side == 0 and p == 0:
            pl.semaphore_wait(barrier, m)
            for item in small[4:6]:
                item.wait()
            for item in far_weights:
                item.start()

        @pl.loop(0, m - 1)
        def _(i):
            copy(p, side, turn(i)).start()

        rows = pl.ds(side * m * cap, cap)
        landed[rows, cols] = packed[rows, cols]

    for p in range(parts):
        pieces[p].wait()
        start_part(0, p)
        if p == 0:
            block = trace_count // block_ref.shape[1]
            spot = iota((1, trace_count), 1)
            trace_class = jnp.zeros((1, trace_count), jnp.int32)
            for b in range(block_ref.shape[1]):
                inside = (spot >= b * block) & (spot < (b + 1) * block)
                value = jnp.broadcast_to(block_ref[:, b : b + 1], (1, trace_count))
                trace_class = jnp.where(inside, value, trace_class)
            ident = (trace_class * share + bins - tile * share).astype(jnp.float32)
            ident = jnp.broadcast_to(to_column(ident), (trace_count, LANES)).astype(jnp.bfloat16)
            for chunk in range(chunks):
                rows = pl.ds(chunk * CHUNK, CHUNK)
                wide = jnp.transpose(dot(pick[rows, :], ident))[0:per_chunk]
                lane = iota((per_chunk, CHUNK), 1)
                first = iota((per_chunk, CHUNK), 0) * cap
                mine = (lane >= first) & (lane < first + cap)
                names_out[pl.ds(chunk * per_chunk, per_chunk), :] = jnp.where(mine, wide, 0.0)

            @pl.loop(0, m - 1)
            def _(i):
                name_copy(0, turn(i)).start()
                name_copy(1, turn(i)).start()

            names_in[0:1] = names_out[0:1]
            names_in[m : m + 1] = names_out[m : m + 1]

    for p in range(parts):
        start_part(1, p)

    position = iota((2 * LANES, LANES), 0) - iota((2 * LANES, LANES), 1)

    def moveout_matrices(side, weights_ref, shifts_ref):
        @pl.loop(0, groups)
        def _(g):
            cols = pl.ds(pl.multiple_of(g * LANES, LANES), LANES)
            for c in range(noff):
                place_rel = position - shifts_ref[c : c + 1, cols]
                weights = weights_ref[c * taps : (c + 1) * taps, cols].astype(jnp.float32)
                matrix = jnp.zeros((2 * LANES, LANES), jnp.float32)
                for b in range(taps):
                    matrix = jnp.where(place_rel == b, weights[b : b + 1], matrix)
                nmo[side, g * noff + c] = matrix.astype(jnp.bfloat16)

    for item in far_weights:
        item.wait_recv()
    moveout_matrices(0, coef_in, shift_in)

    for c in range(noff):
        halves[c, :, pl.ds(length, LANES)] = jnp.zeros((2 * share, LANES), jnp.bfloat16)
    scale = 1.0 / to_column(fold_ref[...].astype(jnp.float32))

    @pl.loop(1, m)
    def _(k):
        name_copy(0, k).wait_recv()
        name_copy(1, k).wait_recv()

    for chunk in range(chunks):
        row = jnp.sum(names_in[pl.ds(chunk * per_chunk, per_chunk), :], 0, keepdims=True)
        hit = iota((ids, CHUNK), 0).astype(jnp.float32) == row
        chosen[:, pl.ds(chunk * CHUNK, CHUNK)] = jnp.where(hit, 1.0, 0.0).astype(jnp.bfloat16)

    def sums(side, p):
        @pl.loop(1, m)
        def _(k):
            copy(p, side, k).wait_recv()

        step = 2 * LANES
        rows = pl.ds(side * m * cap, m * cap)
        for j in range(width // step):
            cols = pl.ds(p * width + j * step, step)
            high, low = split(dot(chosen[:, rows], landed[rows, cols]))
            for c in range(noff):
                halves[c, 0:share, cols] = high[c * share : (c + 1) * share]
                halves[c, share : 2 * share, cols] = low[c * share : (c + 1) * share]

    def moveout(side, g):
        acc = dot(halves[0, :, pl.ds(g * LANES, 2 * LANES)], nmo[side, g * noff])
        for c in range(1, noff):
            acc = acc + dot(halves[c, :, pl.ds(g * LANES, 2 * LANES)], nmo[side, g * noff + c])
        return acc[0:share] + acc[share:]

    for p in range(parts):
        sums(0, p)
        for g in range(starts[p], ends[p]):
            sums_out[:, pl.ds(g * LANES, LANES)] = moveout(0, g)
        far_sums[p].start()

    moveout_matrices(1, coef, shift)
    small[6].wait()

    @pl.loop(0, groups)
    def _(g):
        cols = pl.ds(pl.multiple_of(g * LANES, LANES), LANES)
        matrix = jnp.zeros((2 * LANES, LANES), jnp.float32)
        for b in range(filter_taps):
            matrix = jnp.where(position == LANES // 2 + b - half, band[b : b + 1, cols], matrix)
        high, low = split(matrix)
        bp_high[g] = high
        bp_low[g] = low

    left = iota((share, LANES), 1) < LANES // 2

    def store_shifted(g, value):
        high, low = split(value)
        cols = pl.ds(g * LANES, LANES)
        shifted[0:share, cols] = high
        shifted[share : 2 * share, cols] = low

    def bandpass(g):
        window = shifted[:, pl.ds(g * LANES, 2 * LANES)]
        first = dot(window, bp_high[g])
        second = dot(window[0:share], bp_low[g])
        out[:, pl.ds(g * LANES, LANES)] = (first[0:share] + first[share:] + second) * scale

    before = jnp.zeros((share, LANES), jnp.float32)
    for p in range(parts):
        sums(1, p)
        mine = [moveout(1, g) for g in range(starts[p], ends[p])]
        far_sums[p].wait_recv()
        for g in range(starts[p], ends[p]):
            whole = mine[g - starts[p]] + sums_in[:, pl.ds(g * LANES, LANES)]
            turned = pltpu.roll(whole, LANES // 2, 1)
            store_shifted(g, jnp.where(left, before, turned))
            before = turned
            if g >= 1:
                bandpass(g - 1)
    store_shifted(groups, jnp.where(left, before, 0.0))
    bandpass(groups - 1)

    for item in far_weights + far_sums:
        item.wait_send()

    @pl.loop(1, m)
    def _(k):
        for side in (0, 1):
            name_copy(side, k).wait_send()
            for p in range(parts):
                copy(p, side, k).wait_send()


def body(traces, trace_line, trace_bin, block_offset, nmo_coef, band_shift, bandpass, fold):
    n_line = lax.axis_size("line")
    n_tile = lax.axis_size("tile")
    n = n_line * n_tile
    trace_count, length = traces.shape
    share = fold.shape[1]
    noff, taps = nmo_coef.shape[1:3]
    groups = length // LANES
    cap = -(-(2 * trace_count // n) // 16) * 16
    rows = n * cap
    parts = PARTS
    vmem = pl.BlockSpec(memory_space=pltpu.VMEM)
    hbm = pl.BlockSpec(memory_space=pltpu.HBM)
    result = pl.pallas_call(
        functools.partial(kernel, n_line, n_tile, cap, noff, taps),
        out_shape=jax.ShapeDtypeStruct((share, length), jnp.float32),
        in_specs=[hbm] * 8,
        out_specs=vmem,
        scratch_shapes=[
            pltpu.VMEM((trace_count, length), jnp.bfloat16),
            pltpu.VMEM((1, trace_count), jnp.int32),
            pltpu.VMEM((1, trace_count), jnp.int32),
            pltpu.VMEM((1, block_offset.shape[0]), jnp.int32),
            pltpu.VMEM((noff * taps, length), jnp.bfloat16),
            pltpu.VMEM((noff, length), jnp.int32),
            pltpu.VMEM(bandpass.shape, jnp.float32),
            pltpu.VMEM((1, share), jnp.int32),
            pltpu.VMEM((rows, trace_count), jnp.bfloat16),
            pltpu.VMEM((rows, length), jnp.bfloat16),
            pltpu.VMEM((rows, length), jnp.bfloat16),
            pltpu.VMEM((n, LANES), jnp.float32),
            pltpu.VMEM((n, LANES), jnp.float32),
            pltpu.VMEM((noff * share, rows), jnp.bfloat16),
            pltpu.VMEM((noff, 2 * share, length + LANES), jnp.bfloat16),
            pltpu.VMEM((2, groups * noff, 2 * LANES, LANES), jnp.bfloat16),
            pltpu.VMEM((groups, 2 * LANES, LANES), jnp.bfloat16),
            pltpu.VMEM((groups, 2 * LANES, LANES), jnp.bfloat16),
            pltpu.VMEM((2 * share, length + LANES), jnp.bfloat16),
            pltpu.VMEM((noff * taps, length), jnp.bfloat16),
            pltpu.VMEM((noff, length), jnp.int32),
            pltpu.VMEM((share, length), jnp.float32),
            pltpu.VMEM((share, length), jnp.float32),
            pltpu.SemaphoreType.DMA((7,)),
            pltpu.SemaphoreType.DMA((parts,)),
            pltpu.SemaphoreType.DMA((parts, n)),
            pltpu.SemaphoreType.DMA((parts, n)),
            pltpu.SemaphoreType.DMA((n,)),
            pltpu.SemaphoreType.DMA((n,)),
            pltpu.SemaphoreType.DMA((parts + 2,)),
            pltpu.SemaphoreType.DMA((parts + 2,)),
        ],
        compiler_params=pltpu.CompilerParams(
            collective_id=0, has_side_effects=True, vmem_limit_bytes=60 * 1024 * 1024
        ),
        name="route_and_stack",
    )(
        traces,
        trace_line.reshape(1, -1),
        trace_bin.reshape(1, -1),
        block_offset.reshape(1, -1),
        nmo_coef.reshape(noff * taps, length),
        band_shift.reshape(noff, length),
        bandpass,
        fold,
    )
    return result[None]


def solution(mesh):
    placed = (
        P(("line", "tile"), None),
        P(("line", "tile")),
        P(("line", "tile")),
        P(("line", "tile")),
        P("line", None, None, None),
        P("line", None, None),
        P(),
        P("line", "tile"),
    )
    return jax.shard_map(
        body, mesh=mesh, in_specs=placed, out_specs=P("line", "tile", None), check_vma=False
    )
```

```python
import functools

import jax
import jax.numpy as jnp
from jax import lax
from jax.experimental import pallas as pl
from jax.experimental.pallas import tpu as pltpu
from jax.sharding import PartitionSpec as P

LANES = 128
CHUNK = 128
PARTS = 2
MESH = pl.DeviceIdType.MESH


def iota(shape, dim):
    return lax.broadcasted_iota(jnp.int32, shape, dim)


def to_column(row):
    n = row.shape[1]
    wide = jnp.broadcast_to(row, (n, n))
    return jnp.sum(jnp.where(iota((n, n), 0) == iota((n, n), 1), wide, 0.0), 1, keepdims=True)


def dot(a, b):
    return jnp.dot(a, b, preferred_element_type=jnp.float32)


def split(value):
    high = value.astype(jnp.bfloat16)
    low = (value - high.astype(jnp.float32)).astype(jnp.bfloat16)
    return high, low


def kernel(
    n_line, n_tile, cap, noff, taps,
    traces_hbm, line_hbm, bin_hbm, block_hbm, coef_hbm, shift_hbm, band_hbm, fold_hbm,
    out,
    traces, line_ref, bin_ref, block_ref, coef, shift, band, fold_ref,
    pick, packed, landed, names_out, names_in, chosen, halves, nmo, bp_high, bp_low, shifted,
    coef_in, shift_in, sums_out, sums_in,
    local_sem, part_sem, send_sem, recv_sem, name_send_sem, name_recv_sem,
    far_send_sem, far_recv_sem,
):
    n = n_line * n_tile
    me = lax.axis_index("line") * n_tile + lax.axis_index("tile")
    m = n // 2
    my_half = me // m
    spot_in_half = me % m
    trace_count, length = traces.shape
    share = out.shape[0]
    ids = noff * share
    groups = length // LANES
    per_chunk = CHUNK // cap
    chunks = n // per_chunk
    parts = part_sem.shape[0]
    width = length // parts
    filter_taps = band.shape[0]
    half = (filter_taps - 1) // 2

    small = [
        pltpu.make_async_copy(source, target, local_sem.at[index])
        for index, (source, target) in enumerate(
            [
                (line_hbm, line_ref), (bin_hbm, bin_ref), (block_hbm, block_ref),
                (fold_hbm, fold_ref), (shift_hbm, shift), (coef_hbm, coef), (band_hbm, band),
            ]
        )
    ]
    for item in small[:4]:
        item.start()
    pieces = []
    for p in range(parts):
        cols = pl.ds(p * width, width)
        pieces.append(
            pltpu.make_async_copy(traces_hbm.at[:, cols], traces.at[:, cols], part_sem.at[p])
        )
        pieces[p].start()
    for item in small[4:]:
        item.start()

    def place(index):
        return (index // n_tile, index % n_tile)

    barrier = pltpu.get_barrier_semaphore()

    mirror = place((me + m) % n)

    def peer(k):
        return place(my_half * m + (spot_in_half + k) % m)

    @pl.loop(1, m)
    def _(k):
        pl.semaphore_signal(barrier, inc=1, device_id=peer(k), device_id_type=MESH)

    pl.semaphore_signal(barrier, inc=1, device_id=mirror, device_id_type=MESH)

    for item in small[:4]:
        item.wait()

    bins = bin_ref[...]
    tile = jnp.zeros_like(bins)
    for t in range(1, n_tile):
        tile = tile + jnp.where(bins >= t * share, 1, 0)
    owner = line_ref[...] * n_tile + tile
    owner_half = jnp.where(owner >= m, 1, 0)
    offset = owner - owner_half * m - spot_in_half
    offset = jnp.where(offset < 0, offset + m, offset)
    offset = jnp.where(owner_half == my_half, offset + m, offset).astype(jnp.float32)
    same = (to_column(offset) == offset) & (
        iota((trace_count, trace_count), 0) < iota((trace_count, trace_count), 1)
    )
    rank = jnp.sum(jnp.where(same, 1.0, 0.0), 0, keepdims=True)
    slot = offset * cap + rank

    for chunk in range(chunks):
        rows = (iota((CHUNK, trace_count), 0) + chunk * CHUNK).astype(jnp.float32)
        pick[pl.ds(chunk * CHUNK, CHUNK), :] = jnp.where(rows == slot, 1.0, 0.0).astype(jnp.bfloat16)

    def copy(p, side, k):
        rows = pl.ds(pl.multiple_of((side * m + k) * cap, cap), cap)
        cols = pl.ds(p * width, width)
        return pltpu.make_async_remote_copy(
            src_ref=packed.at[rows, cols],
            dst_ref=landed.at[rows, cols],
            send_sem=send_sem.at[p, side * m + k],
            recv_sem=recv_sem.at[p, side * m + k],
            device_id=peer(k),
            device_id_type=MESH,
        )

    def name_copy(side, k):
        index = side * m + k
        return pltpu.make_async_remote_copy(
            src_ref=names_out.at[pl.ds(index, 1)],
            dst_ref=names_in.at[pl.ds(index, 1)],
            send_sem=name_send_sem.at[index],
            recv_sem=name_recv_sem.at[index],
            device_id=peer(k),
            device_id_type=MESH,
        )

    def far_copy(index, source, target):
        return pltpu.make_async_remote_copy(
            src_ref=source,
            dst_ref=target,
            send_sem=far_send_sem.at[index],
            recv_sem=far_recv_sem.at[index],
            device_id=mirror,
            device_id_type=MESH,
        )

    far_weights = [far_copy(parts, shift, shift_in), far_copy(parts + 1, coef, coef_in)]

    ends = [(p + 1) * width // LANES - 1 for p in range(parts - 1)] + [groups]
    starts = [0] + ends[:-1]
    far_sums = []
    for p in range(parts):
        cols = pl.ds(starts[p] * LANES, (ends[p] - starts[p]) * LANES)
        far_sums.append(far_copy(p, sums_out.at[:, cols], sums_in.at[:, cols]))

    def turn(i):
        return 1 + (i + m // 2 - 1) % (m - 1)

    def start_part(side, p):
        cols = pl.ds(p * width, width)

        @pl.loop(0, chunks // 2)
        def _(chunk):
            rows = pl.ds(pl.multiple_of((side * (chunks // 2) + chunk) * CHUNK, CHUNK), CHUNK)
            packed[rows, cols] = dot(pick[rows, :], traces[:, cols]).astype(jnp.bfloat16)

        if side == 0 and p == 0:
            pl.semaphore_wait(barrier, m)
            for item in small[4:6]:
                item.wait()
            for item in far_weights:
                item.start()

        @pl.loop(0, m - 1)
        def _(i):
            copy(p, side, turn(i)).start()

        rows = pl.ds(side * m * cap, cap)
        landed[rows, cols] = packed[rows, cols]

    for p in range(parts):
        pieces[p].wait()
        start_part(0, p)
        if p == 0:
            block = trace_count // block_ref.shape[1]
            spot = iota((1, trace_count), 1)
            trace_class = jnp.zeros((1, trace_count), jnp.int32)
            for b in range(block_ref.shape[1]):
                inside = (spot >= b * block) & (spot < (b + 1) * block)
                value = jnp.broadcast_to(block_ref[:, b : b + 1], (1, trace_count))
                trace_class = jnp.where(inside, value, trace_class)
            ident = (trace_class * share + bins - tile * share).astype(jnp.float32)
            ident = jnp.broadcast_to(to_column(ident), (trace_count, LANES)).astype(jnp.bfloat16)
            for chunk in range(chunks):
                rows = pl.ds(chunk * CHUNK, CHUNK)
                wide = jnp.transpose(dot(pick[rows, :], ident))[0:per_chunk]
                lane = iota((per_chunk, CHUNK), 1)
                first = iota((per_chunk, CHUNK), 0) * cap
                mine = (lane >= first) & (lane < first + cap)
                names_out[pl.ds(chunk * per_chunk, per_chunk), :] = jnp.where(mine, wide, 0.0)

            @pl.loop(0, m - 1)
            def _(i):
                name_copy(0, turn(i)).start()
                name_copy(1, turn(i)).start()

            names_in[0:1] = names_out[0:1]
            names_in[m : m + 1] = names_out[m : m + 1]

    for p in range(parts):
        start_part(1, p)

    position = iota((2 * LANES, LANES), 0) - iota((2 * LANES, LANES), 1)

    def moveout_matrices(side, weights_ref, shifts_ref):
        @pl.loop(0, groups)
        def _(g):
            cols = pl.ds(pl.multiple_of(g * LANES, LANES), LANES)
            for c in range(noff):
                place_rel = position - shifts_ref[c : c + 1, cols]
                weights = weights_ref[c * taps : (c + 1) * taps, cols].astype(jnp.float32)
                matrix = jnp.zeros((2 * LANES, LANES), jnp.float32)
                for b in range(taps):
                    matrix = jnp.where(place_rel == b, weights[b : b + 1], matrix)
                nmo[side, g * noff + c] = matrix.astype(jnp.bfloat16)

    for item in far_weights:
        item.wait_recv()
    moveout_matrices(0, coef_in, shift_in)

    for c in range(noff):
        halves[c, :, pl.ds(length, LANES)] = jnp.zeros((2 * share, LANES), jnp.bfloat16)
    scale = 1.0 / to_column(fold_ref[...].astype(jnp.float32))

    @pl.loop(1, m)
    def _(k):
        name_copy(0, k).wait_recv()
        name_copy(1, k).wait_recv()

    for chunk in range(chunks):
        row = jnp.sum(names_in[pl.ds(chunk * per_chunk, per_chunk), :], 0, keepdims=True)
        hit = iota((ids, CHUNK), 0).astype(jnp.float32) == row
        chosen[:, pl.ds(chunk * CHUNK, CHUNK)] = jnp.where(hit, 1.0, 0.0).astype(jnp.bfloat16)

    def sums(side, p):
        @pl.loop(1, m)
        def _(k):
            copy(p, side, k).wait_recv()

        step = 2 * LANES
        rows = pl.ds(side * m * cap, m * cap)
        for j in range(width // step):
            cols = pl.ds(p * width + j * step, step)
            high, low = split(dot(chosen[:, rows], landed[rows, cols]))
            for c in range(noff):
                halves[c, 0:share, cols] = high[c * share : (c + 1) * share]
                halves[c, share : 2 * share, cols] = low[c * share : (c + 1) * share]

    def moveout(side, g):
        acc = dot(halves[0, :, pl.ds(g * LANES, 2 * LANES)], nmo[side, g * noff])
        for c in range(1, noff):
            acc = acc + dot(halves[c, :, pl.ds(g * LANES, 2 * LANES)], nmo[side, g * noff + c])
        return acc[0:share] + acc[share:]

    for p in range(parts):
        sums(0, p)
        for g in range(starts[p], ends[p]):
            sums_out[:, pl.ds(g * LANES, LANES)] = moveout(0, g)
        far_sums[p].start()

    moveout_matrices(1, coef, shift)
    small[6].wait()

    @pl.loop(0, groups)
    def _(g):
        cols = pl.ds(pl.multiple_of(g * LANES, LANES), LANES)
        matrix = jnp.zeros((2 * LANES, LANES), jnp.float32)
        for b in range(filter_taps):
            matrix = jnp.where(position == LANES // 2 + b - half, band[b : b + 1, cols], matrix)
        high, low = split(matrix)
        bp_high[g] = high
        bp_low[g] = low

    left = iota((share, LANES), 1) < LANES // 2

    def store_shifted(g, value):
        high, low = split(value)
        cols = pl.ds(g * LANES, LANES)
        shifted[0:share, cols] = high
        shifted[share : 2 * share, cols] = low

    def bandpass(g):
        window = shifted[:, pl.ds(g * LANES, 2 * LANES)]
        first = dot(window, bp_high[g])
        second = dot(window[0:share], bp_low[g])
        out[:, pl.ds(g * LANES, LANES)] = (first[0:share] + first[share:] + second) * scale

    before = jnp.zeros((share, LANES), jnp.float32)
    for p in range(parts):
        sums(1, p)
        mine = [moveout(1, g) for g in range(starts[p], ends[p])]
        far_sums[p].wait_recv()
        for g in range(starts[p], ends[p]):
            whole = mine[g - starts[p]] + sums_in[:, pl.ds(g * LANES, LANES)]
            turned = pltpu.roll(whole, LANES // 2, 1)
            store_shifted(g, jnp.where(left, before, turned))
            before = turned
            if g >= 1:
                bandpass(g - 1)
    store_shifted(groups, jnp.where(left, before, 0.0))
    bandpass(groups - 1)

    for item in far_weights + far_sums:
        item.wait_send()

    @pl.loop(1, m)
    def _(k):
        for side in (0, 1):
            name_copy(side, k).wait_send()
            for p in range(parts):
                copy(p, side, k).wait_send()


def body(traces, trace_line, trace_bin, block_offset, nmo_coef, band_shift, bandpass, fold):
    n_line = lax.axis_size("line")
    n_tile = lax.axis_size("tile")
    n = n_line * n_tile
    trace_count, length = traces.shape
    share = fold.shape[1]
    noff, taps = nmo_coef.shape[1:3]
    groups = length // LANES
    cap = -(-(2 * trace_count // n) // 16) * 16
    rows = n * cap
    parts = PARTS
    vmem = pl.BlockSpec(memory_space=pltpu.VMEM)
    hbm = pl.BlockSpec(memory_space=pltpu.HBM)
    result = pl.pallas_call(
        functools.partial(kernel, n_line, n_tile, cap, noff, taps),
        out_shape=jax.ShapeDtypeStruct((share, length), jnp.float32),
        in_specs=[hbm] * 8,
        out_specs=vmem,
        scratch_shapes=[
            pltpu.VMEM((trace_count, length), jnp.bfloat16),
            pltpu.VMEM((1, trace_count), jnp.int32),
            pltpu.VMEM((1, trace_count), jnp.int32),
            pltpu.VMEM((1, block_offset.shape[0]), jnp.int32),
            pltpu.VMEM((noff * taps, length), jnp.bfloat16),
            pltpu.VMEM((noff, length), jnp.int32),
            pltpu.VMEM(bandpass.shape, jnp.float32),
            pltpu.VMEM((1, share), jnp.int32),
            pltpu.VMEM((rows, trace_count), jnp.bfloat16),
            pltpu.VMEM((rows, length), jnp.bfloat16),
            pltpu.VMEM((rows, length), jnp.bfloat16),
            pltpu.VMEM((n, LANES), jnp.float32),
            pltpu.VMEM((n, LANES), jnp.float32),
            pltpu.VMEM((noff * share, rows), jnp.bfloat16),
            pltpu.VMEM((noff, 2 * share, length + LANES), jnp.bfloat16),
            pltpu.VMEM((2, groups * noff, 2 * LANES, LANES), jnp.bfloat16),
            pltpu.VMEM((groups, 2 * LANES, LANES), jnp.bfloat16),
            pltpu.VMEM((groups, 2 * LANES, LANES), jnp.bfloat16),
            pltpu.VMEM((2 * share, length + LANES), jnp.bfloat16),
            pltpu.VMEM((noff * taps, length), jnp.bfloat16),
            pltpu.VMEM((noff, length), jnp.int32),
            pltpu.VMEM((share, length), jnp.float32),
            pltpu.VMEM((share, length), jnp.float32),
            pltpu.SemaphoreType.DMA((7,)),
            pltpu.SemaphoreType.DMA((parts,)),
            pltpu.SemaphoreType.DMA((parts, n)),
            pltpu.SemaphoreType.DMA((parts, n)),
            pltpu.SemaphoreType.DMA((n,)),
            pltpu.SemaphoreType.DMA((n,)),
            pltpu.SemaphoreType.DMA((parts + 2,)),
            pltpu.SemaphoreType.DMA((parts + 2,)),
        ],
        compiler_params=pltpu.CompilerParams(
            collective_id=0, has_side_effects=True, vmem_limit_bytes=60 * 1024 * 1024
        ),
        name="route_and_stack",
    )(
        traces,
        trace_line.reshape(1, -1),
        trace_bin.reshape(1, -1),
        block_offset.reshape(1, -1),
        nmo_coef.reshape(noff * taps, length),
        band_shift.reshape(noff, length),
        bandpass,
        fold,
    )
    return result[None]


def solution(mesh):
    placed = (
        P(("line", "tile"), None),
        P(("line", "tile")),
        P(("line", "tile")),
        P(("line", "tile")),
        P("line", None, None, None),
        P("line", None, None),
        P(),
        P("line", "tile"),
    )
    return jax.shard_map(
        body, mesh=mesh, in_specs=placed, out_specs=P("line", "tile", None), check_vma=False
    )
```
